32 devices in a mesh: dp: 4 (over z), ctx: 2 (over x), tensor: 4 (over y, core).
Axes of the slice: x: 2, y: 2, z: 4, core: 2. Of those that a mesh axis runs over, the one named last changes fastest.
Arguments:
- tokens: bfloat16 [4, 2048, 1024], P('dp', 'ctx'), may hold values from -6 to 6
- first_gain: float32 [1024], replicated, may hold values from 0.5 to 1.5
- query_weight: bfloat16 [1024, 1024], P(None, 'tensor'), may hold values from -0.1875 to 0.1875
- key_weight: bfloat16 [1024, 1024], P(None, 'tensor'), may hold values from -0.1875 to 0.1875
- value_weight: bfloat16 [1024, 2048], P(None, 'tensor'), may hold values from -0.1875 to 0.1875
- outgate_weight: bfloat16 [1024, 2048], P(None, 'tensor'), may hold values from -0.1875 to 0.1875
- alpha_weight: bfloat16 [1024, 8], P(None, 'tensor'), may hold values from -0.1875 to 0.1875
- beta_weight: bfloat16 [1024, 8], P(None, 'tensor'), may hold values from -0.1875 to 0.1875
- query_conv: float32 [4, 1024], P(None, 'tensor'), may hold values from -3 to 3
- convolved_keys: float32 [4, 1024], P(None, 'tensor'), may hold values from -3 to 3
- value_conv: float32 [4, 2048], P(None, 'tensor'), may hold values from -3 to 3
- decay_rate: float32 [8], P('tensor'), may hold values from 0.0002 to 0.08
- time_bias: float32 [8], P('tensor'), may hold values from -1 to 1
- head_gain: float32 [256], replicated, may hold values from 0.5 to 1.5
- out_weight: bfloat16 [2048, 1024], P('tensor'), may hold values from -0.25 to 0.25
- second_gain: float32 [1024], replicated, may hold values from 0.5 to 1.5
- gate_weight: bfloat16 [1024, 2816], P(None, 'tensor'), may hold values from -0.1875 to 0.1875
- up_weight: bfloat16 [1024, 2816], P(None, 'tensor'), may hold values from -0.1875 to 0.1875
- down_weight: bfloat16 [2816, 1024], P('tensor'), may hold values from -0.109375 to 0.109375
- cotangent: bfloat16 [4, 2048, 1024], P('dp', 'ctx'), may hold values from -6 to 6
Outputs:
- block_out: bfloat16 [4, 2048, 1024], P('dp', 'ctx')
- tokens_grad: bfloat16 [4, 2048, 1024], P('dp', 'ctx')
- first_gain_grad: float32 [1024], replicated
- query_weight_grad: float32 [1024, 1024], P(('dp', 'ctx'), 'tensor')
- key_weight_grad: float32 [1024, 1024], P(('dp', 'ctx'), 'tensor')
- value_weight_grad: float32 [1024, 2048], P(('dp', 'ctx'), 'tensor')
- outgate_weight_grad: float32 [1024, 2048], P(('dp', 'ctx'), 'tensor')
- alpha_weight_grad: float32 [1024, 8], P(('dp', 'ctx'), 'tensor')
- beta_weight_grad: float32 [1024, 8], P(('dp', 'ctx'), 'tensor')
- query_conv_grad: float32 [4, 1024], P(None, 'tensor')
- key_conv_grad: float32 [4, 1024], P(None, 'tensor')
- value_conv_grad: float32 [4, 2048], P(None, 'tensor')
- decay_rate_grad: float32 [8], P('tensor')
- time_bias_grad: float32 [8], P('tensor')
- head_gain_grad: float32 [256], replicated
- out_weight_grad: float32 [2048, 1024], P('tensor', ('dp', 'ctx'))
- second_gain_grad: float32 [1024], replicated
- gate_weight_grad: float32 [1024, 2816], P(('dp', 'ctx'), 'tensor')
- up_weight_grad: float32 [1024, 2816], P(('dp', 'ctx'), 'tensor')
- down_weight_grad: float32 [2816, 1024], P('tensor', ('dp', 'ctx'))
The draws below stay inside these ranges and needn't reach their ends.
All inputs are finite; a program needn't handle non-finite values.
Results may differ from the reference program's by a relative error of at most 0.038.
Values may be sent and summed in bfloat16 or wider, within the bound.
A program may use at most 192 MiB of HBM per device.

```python
import math
import jax
import jax.numpy as jnp
from jax import lax

D = 1024
H = 8
DK = 128
DV = 256
FF = 2816
KCONV = 4
SPAN = 64
LEN = 2048
NSEQ = 4


def block_levels(key, extent, cuts, smallest, top_value):
    def one(dim, shards_of):
        steps = jax.random.uniform(jax.random.fold_in(jax.random.fold_in(key, 6), dim), (shards_of,), jnp.float32, smallest / len(cuts), top_value / len(cuts))
        return jnp.repeat(jnp.exp(steps), extent[dim] // shards_of).reshape((-1,) + (1,) * (len(extent) - dim - 1))

    gain = one(*cuts[0])
    for cut in cuts[1:]:
        gain = gain * one(*cut)
    return gain


def noise(key, shape, spread, most, cuts=(), kind=jnp.bfloat16):
    drawn = jax.random.normal(key, shape, jnp.float32) * spread
    if len(cuts) > 0:
        drawn = block_levels(key, shape, cuts, -0.22, 0.18) * drawn
    return jnp.clip(drawn, min=-most, max=most).astype(kind)


def setup_inputs(seed: int = 0) -> dict:
    seeds = jax.random.split(jax.random.key(seed), 21)
    return {
        "tokens": noise(seeds[0], (NSEQ, LEN, D), 1.0, 6.0, ((0, 4), (1, 2))),
        "first_gain": jnp.clip(1.0 + 0.1 * jax.random.normal(seeds[1], (D,), jnp.float32), 0.5, 1.5),
        "query_weight": noise(seeds[2], (D, H * DK), D ** -0.5, 0.1875, ((1, 4),)),
        "key_weight": noise(seeds[3], (D, H * DK), D ** -0.5, 0.1875, ((1, 4),)),
        "value_weight": noise(seeds[4], (D, H * DV), D ** -0.5, 0.1875, ((1, 4),)),
        "outgate_weight": noise(seeds[5], (D, H * DV), D ** -0.5, 0.1875, ((1, 4),)),
        "alpha_weight": noise(seeds[6], (D, H), D ** -0.5, 0.1875, ((1, 4),)),
        "beta_weight": noise(seeds[7], (D, H), D ** -0.5, 0.1875, ((1, 4),)),
        "query_conv": noise(seeds[8], (KCONV, H * DK), KCONV ** -0.5, 3.0, ((1, 4),), jnp.float32),
        "convolved_keys": noise(seeds[9], (KCONV, H * DK), KCONV ** -0.5, 3.0, ((1, 4),), jnp.float32),
        "value_conv": noise(seeds[10], (KCONV, H * DV), KCONV ** -0.5, 3.0, ((1, 4),), jnp.float32),
        "decay_rate": jnp.clip(jnp.exp(math.log(0.08) - 5.9914646 * jax.random.uniform(seeds[11], (H,), jnp.float32) ** block_levels(seeds[11], (H,), ((0, 4),), -0.2, 0.2)), 0.0002, 0.08),
        "time_bias": jnp.clip(jax.random.uniform(seeds[12], (H,), jnp.float32, -1.0, 1.0) * block_levels(seeds[12], (H,), ((0, 4),), -0.4, 0.0), -1.0, 1.0),
        "head_gain": jnp.clip(1.0 + 0.1 * jax.random.normal(seeds[13], (DV,), jnp.float32), 0.5, 1.5),
        "out_weight": noise(seeds[14], (H * DV, D), (H * DV // 4) ** -0.5, 0.25, ((0, 4),)),
        "second_gain": jnp.clip(1.0 + 0.1 * jax.random.normal(seeds[15], (D,), jnp.float32), 0.5, 1.5),
        "gate_weight": noise(seeds[16], (D, FF), D ** -0.5, 0.1875, ((1, 4),)),
        "up_weight": noise(seeds[17], (D, FF), D ** -0.5, 0.1875, ((1, 4),)),
        "down_weight": noise(seeds[18], (FF, D), FF ** -0.5, 0.109375, ((0, 4),)),
        "cotangent": noise(seeds[19], (NSEQ, LEN, D), 1.0, 6.0, ((0, 4), (1, 2))),
    }


@jax.custom_vjp
def low(v):
    return lax.optimization_barrier(v.astype(jnp.bfloat16)).astype(jnp.float32)

@jax.custom_vjp
def low_back(v):
    return v

def low_keep(v):
    return (low(v), None)

def low_pass(kept, grad):
    return (grad,)

def back_keep(v):
    return (v, None)

def back_low(kept, grad):
    return (low(grad),)
low.defvjp(low_keep, low_pass)
low_back.defvjp(back_keep, back_low)
epsilon = 1e-06
maximal_precision = lax.Precision.HIGHEST

def high_dot(left, right):
    return jnp.matmul(left, right, precision=maximal_precision)

def rms_gain(rows_in, gain_in):
    return rows_in * lax.rsqrt(lax.optimization_barrier(jnp.mean(rows_in * rows_in, -1, keepdims=True)) + epsilon) * gain_in

def gated_out(head_vals, gate_vals, gain_in):
    return rms_gain(head_vals, gain_in) * jax.nn.silu(gate_vals)

def short_conv(linear, kernel):
    padded = jnp.pad(linear, ((KCONV - 1, 0), (0, 0)))
    summed = sum((kernel[tap_index] * padded[tap_index:tap_index + LEN] for tap_index in range(KCONV)))
    return jax.nn.silu(summed)

def unit_rows(block_in):
    return block_in * lax.rsqrt(lax.optimization_barrier(jnp.sum(block_in * block_in, -1, keepdims=True)) + epsilon)

def delta_rule(queries, keys_in, values_in, log_gate, strength):

    def token_step(recurrent_state, token_in):
        current_query, current_key, value_now, gate_now, beta_now = token_in
        retain = jnp.exp(gate_now)
        prediction_value = jnp.einsum('yop,yo->yp', recurrent_state, current_key, precision=maximal_precision)
        update = beta_now[:, None] * (value_now - retain[:, None] * prediction_value)
        recurrent_state = retain[:, None, None] * recurrent_state + current_key[:, :, None] * update[:, None, :]
        return (recurrent_state, jnp.einsum('yop,yo->yp', recurrent_state, current_query, precision=maximal_precision))

    @jax.checkpoint
    def block_step(recurrent_state, block_in):
        return lax.scan(token_step, recurrent_state, block_in)
    blocks = tuple((item.reshape((LEN // SPAN, SPAN) + item.shape[1:]) for item in (queries, keys_in, values_in, log_gate, strength)))
    initial = jnp.zeros((H, DK, DV), jnp.float32)
    unused, outputs = lax.scan(block_step, initial, blocks)
    return outputs.reshape(LEN, H, DV)

def layer(params, rows_in):
    first_gain, query_weight, key_weight, value_weight, outgate_weight, alpha_weight, beta_weight, query_conv, convolved_keys, value_conv, decay_rate, time_bias, head_gain, out_weight, second_gain, gate_weight, up_weight, down_weight = params
    normed1 = low(rms_gain(rows_in, first_gain))

    def project(weight):
        return high_dot(normed1, weight)
    query_lin = low(low_back(project(query_weight)))
    key_lin = low(low_back(project(key_weight)))
    value_lin = low(low_back(project(value_weight)))
    gate_lin = low_back(project(outgate_weight))
    alpha_lin = low_back(project(alpha_weight))
    beta_lin = low_back(project(beta_weight))
    raw_query = short_conv(query_lin, query_conv).reshape(LEN, H, DK)
    raw_key = short_conv(key_lin, convolved_keys).reshape(LEN, H, DK)
    raw_value = short_conv(value_lin, value_conv).reshape(LEN, H, DV)
    queries = low(unit_rows(raw_query) * DK ** (-0.5))
    keys_in = low(unit_rows(raw_key))
    values_in = low(raw_value)
    log_gate = -decay_rate * jax.nn.softplus(alpha_lin + time_bias)
    strength = jax.nn.sigmoid(beta_lin)
    head_out = delta_rule(queries, keys_in, values_in, log_gate, strength)
    normed_heads = low(gated_out(head_out, gate_lin.reshape(LEN, H, DV), head_gain).reshape(LEN, H * DV))
    middle = rows_in + low_back(high_dot(normed_heads, out_weight))
    normed2 = low(rms_gain(middle, second_gain))
    gate_pre = low_back(high_dot(normed2, gate_weight))
    up_pre = low_back(high_dot(normed2, up_weight))
    hidden = low(jax.nn.silu(gate_pre) * up_pre)
    return middle + high_dot(hidden, down_weight)

def reference(tokens, first_gain, query_weight, key_weight, value_weight, outgate_weight, alpha_weight, beta_weight, query_conv, convolved_keys, value_conv, decay_rate, time_bias, head_gain, out_weight, second_gain, gate_weight, up_weight, down_weight, cotangent):
    params = tuple((item.astype(jnp.float32) for item in (first_gain, query_weight, key_weight, value_weight, outgate_weight, alpha_weight, beta_weight, query_conv, convolved_keys, value_conv, decay_rate, time_bias, head_gain, out_weight, second_gain, gate_weight, up_weight, down_weight)))
    initial = tuple((jnp.zeros_like(item) for item in params))

    def per_sequence(totals, paired):
        rows_in, grad_rows = paired
        result, backward = jax.vjp(layer, params, rows_in.astype(jnp.float32))
        param_grads, rows_grad = backward(grad_rows.astype(jnp.float32))
        totals = jax.tree.map(jnp.add, totals, param_grads)
        return (totals, (result.astype(jnp.bfloat16), rows_grad.astype(jnp.bfloat16)))
    totals, outputs = lax.scan(per_sequence, initial, (tokens, cotangent))
    return (outputs[0], outputs[1], totals[0], totals[1], totals[2], totals[3], totals[4], totals[5], totals[6], totals[7], totals[8], totals[9], totals[10], totals[11], totals[12], totals[13], totals[14], totals[15], totals[16], totals[17])
```

```python
import functools

import jax
import jax.numpy as jnp
from jax import lax
from jax.experimental import pallas as pl
from jax.experimental.pallas import tpu as pltpu
from jax.sharding import PartitionSpec as P

KCONV = 4
CHUNK = 128


epsilon = 1e-06
maximal_precision = lax.Precision.HIGHEST


def shifted(value, axis, by):
    devices = lax.axis_size(axis)
    pairs = [(i, i + by) for i in range(devices) if 0 <= i + by < devices]
    return lax.ppermute(value, axis, pairs)


def entering(value, axis, combine, identity, reverse):
    devices, index = (lax.axis_size(axis), lax.axis_index(axis))
    everything = jax.tree.map(
        lambda part, kind: lax.all_gather(part.astype(kind), axis),
        value,
        (jnp.bfloat16, jnp.bfloat16),
    )
    start = jax.tree.map(
        lambda part, zero: jnp.broadcast_to(jnp.asarray(zero, part.dtype), part.shape),
        value,
        identity,
    )

    def lap(k, before):
        at = devices - 1 - k if reverse else k
        reached = at > index if reverse else at < index
        new = combine(
            before, jax.tree.map(lambda part, own: part[at].astype(own.dtype), everything, value)
        )
        return jax.tree.map(lambda a, b: jnp.where(reached, a, b), new, before)

    return lax.fori_loop(0, devices, lap, start)


def high_dot(left, right):
    return jnp.matmul(left, right, precision=maximal_precision)


def flipped(matrix):
    return jnp.swapaxes(matrix, -1, -2)


def span_first(array_in):
    return jnp.moveaxis(array_in, 1, 0)


def rms_gain(rows_in, gain_in):
    return rows_in * lax.rsqrt(jnp.mean(rows_in * rows_in, -1, keepdims=True) + epsilon) * gain_in


def gated_out(head_vals, gate_vals, gain_in):
    return rms_gain(head_vals, gain_in) * jax.nn.silu(gate_vals)


def swiglu(gate_in, up_in):
    return jax.nn.silu(gate_in) * up_in


def dims_dot(left, right, left_dim, right_dim):
    return lax.dot_general(
        left.astype(jnp.bfloat16),
        right.astype(jnp.bfloat16),
        (((left_dim,), (right_dim,)), ((), ())),
        preferred_element_type=jnp.float32,
    )


@jax.custom_vjp
def dot_nn(left, right):
    return dims_dot(left, right, 1, 0)


@jax.custom_vjp
def dot_nt(left, right):
    return dims_dot(left, right, 1, 1)


@jax.custom_vjp
def dot_tn(left, right):
    return dims_dot(left, right, 0, 0)


dot_nn.defvjp(
    lambda l, r: (dims_dot(l, r, 1, 0), (l, r)),
    lambda k, g: (dims_dot(g, k[1], 1, 1), dims_dot(k[0], g, 0, 0)),
)
dot_nt.defvjp(
    lambda l, r: (dims_dot(l, r, 1, 1), (l, r)),
    lambda k, g: (dims_dot(g, k[1], 1, 0), dims_dot(g, k[0], 0, 0)),
)
dot_tn.defvjp(
    lambda l, r: (dims_dot(l, r, 0, 0), (l, r)),
    lambda k, g: (dims_dot(k[1], g, 1, 1), dims_dot(k[0], g, 1, 0)),
)


@jax.custom_vjp
def solve_with(lower, inverse, right):
    return dims_dot(inverse, right, 1, 0)


def solve_fwd(lower, inverse, right):
    found = dims_dot(inverse, right, 1, 0)
    return found, (inverse, found)


def solve_bwd(kept, grad):
    inverse, found = kept
    right_grad = dims_dot(inverse, grad, 0, 0)
    return -dims_dot(right_grad, found, 1, 1), jnp.zeros_like(inverse), right_grad


solve_with.defvjp(solve_fwd, solve_bwd)


def two_parts(value):
    high = value.astype(jnp.bfloat16)
    return high, (value - high.astype(jnp.float32)).astype(jnp.bfloat16)


def grid_indices():
    shape = (CHUNK, CHUNK)
    return lax.broadcasted_iota(jnp.int32, shape, 0), lax.broadcasted_iota(jnp.int32, shape, 1)


def triangle(flip):
    row, col = grid_indices()
    keep = row <= col if flip else row >= col
    return jnp.where(keep, 1.0, 0.0).astype(jnp.bfloat16)


def tri_dot(value, flip):
    tri = triangle(flip)
    high, rest = two_parts(value)
    return dims_dot(tri, high, 1, 0) + dims_dot(tri, rest, 1, 0)


@jax.custom_vjp
def running(value):
    return tri_dot(value, False)


running.defvjp(lambda v: (tri_dot(v, False), None), lambda k, g: (tri_dot(g, True),))


def dot_three(left, right):
    left_high, left_rest = two_parts(left)
    right_high, right_rest = two_parts(right)
    return (
        dims_dot(left_high, right_high, 1, 0)
        + dims_dot(left_high, right_rest, 1, 0)
        + dims_dot(left_rest, right_high, 1, 0)
    )


def unit_inverse(lowers):
    row, col = grid_indices()
    eye = jnp.where(row == col, 1.0, 0.0)
    found = None
    size = 1
    while size < CHUNK:
        pair = (
            (row // (2 * size) == col // (2 * size))
            & (row % (2 * size) >= size)
            & (col % (2 * size) < size)
        )
        corners = [jnp.where(pair, lower, 0.0) for lower in lowers]
        if found is None:
            found = [eye - corner for corner in corners]
        else:
            inner = [dot_three(x, c) for x, c in zip(found, corners)]
            found = [x - dot_three(i, x) for x, i in zip(found, inner)]
        size *= 2
    return found


def decay_parts(gate):
    row, col = grid_indices()
    total = running(gate * jnp.ones((CHUNK, CHUNK), jnp.float32))
    causal = row >= col
    ratio = total - total.T
    decays = jnp.where(causal, jnp.exp(jnp.where(causal, ratio, 0.0)), 0.0)
    last = jnp.sum(jnp.where(row == CHUNK - 1, total, 0.0), 0, keepdims=True)
    tails = jnp.exp(last - total)
    whole = jnp.exp(jnp.sum(gate, 0, keepdims=True))
    return decays, jnp.exp(total), tails, whole


def lower_of(decays, keys, strength):
    row, col = grid_indices()
    return jnp.where(row > col, decays * dot_nt(keys, keys), 0.0) * strength


def chunk_out(queries, keys, values, gate, strength, inverse, state):
    decays, gammas, tails, whole = decay_parts(gate)
    lower = lower_of(decays, keys, strength)
    right = strength * (values - dot_nn(gammas * keys, state))
    fresh = solve_with(lower, inverse, right)
    out = dot_nn(gammas * queries, state) + dot_nn(decays * dot_nt(queries, keys), fresh)
    return out, whole * state + dot_tn(tails * keys, fresh)


def forward_kernel(
    heads, dk, dv, steps,
    q_ref, k_ref, v_ref, gb_ref,
    em_ref, ep_ref, out_ref, inv_ref, mt_ref, s_ref, p_ref, dmap_ref, dadd_ref,
    state, prod,
):
    step = pl.program_id(1)

    @pl.when(step == 0)
    def _():
        row, col = grid_indices()
        state[...] = jnp.zeros_like(state)
        for h in range(heads):
            prod[h] = jnp.where(row == col, 1.0, 0.0)

    parts, lowers = [], []
    for h in range(heads):
        q = q_ref[0, :, h * dk : (h + 1) * dk].astype(jnp.float32)
        k = k_ref[0, :, h * dk : (h + 1) * dk].astype(jnp.float32)
        v = v_ref[0, :, h * dv : (h + 1) * dv].astype(jnp.float32)
        gate = gb_ref[0, h, :, 0:1]
        strength = gb_ref[0, h, :, 1:2]
        decays, gammas, tails, whole = decay_parts(gate)
        lowers.append(lower_of(decays, k, strength))
        parts.append((q, k, v, strength, decays, gammas, tails, whole))
    inverses = unit_inverse(lowers)
    for h in range(heads):
        q, k, v, strength, decays, gammas, tails, whole = parts[h]
        inverse = inverses[h].astype(jnp.bfloat16)
        key_solve = dot_nn(inverse, strength * gammas * k)
        value_solve = dot_nn(inverse, strength * v)
        mixing = decays * dot_nt(q, k)
        emitted = (gammas * q - dot_nn(mixing, key_solve)).astype(jnp.bfloat16)
        tail_keys = tails * k
        minus = dot_tn(tail_keys, key_solve).astype(jnp.bfloat16)
        now_s, now_p = state[h], prod[h]
        inv_ref[0, 0, h] = inverse
        mt_ref[0, 0, h] = minus
        s_ref[0, 0, h] = now_s.astype(jnp.bfloat16)
        p_ref[0, 0, h] = now_p.astype(jnp.bfloat16)
        em_ref[0, :, h * dk : (h + 1) * dk] = emitted
        ep_ref[0, :, h * dk : (h + 1) * dk] = dot_nn(emitted, now_p).astype(jnp.bfloat16)
        out_ref[0, :, h * dv : (h + 1) * dv] = dot_nn(mixing, value_solve) + dot_nn(emitted, now_s)
        new_s = whole * now_s - dot_nn(minus, now_s) + dot_tn(tail_keys, value_solve)
        new_p = whole * now_p - dot_nn(minus, now_p)
        state[h] = new_s
        prod[h] = new_p

        @pl.when(step == steps - 1)
        def _():
            dmap_ref[0, h] = new_p
            dadd_ref[0, h] = new_s


def pull_kernel(
    heads, dk, dv, steps,
    em_ref, mt_ref, gb_ref, grad_ref,
    g_ref, r_ref, pull_ref,
    total, prod,
):
    step = pl.program_id(1)

    @pl.when(step == 0)
    def _():
        row, col = grid_indices()
        total[...] = jnp.zeros_like(total)
        for h in range(heads):
            prod[h] = jnp.where(row == col, 1.0, 0.0)

    for h in range(heads):
        whole = jnp.exp(jnp.sum(gb_ref[0, h, :, 0:1], 0, keepdims=True))
        now_g, now_r = total[h], prod[h]
        g_ref[0, 0, h] = now_g.astype(jnp.bfloat16)
        r_ref[0, 0, h] = now_r.astype(jnp.bfloat16)
        minus = mt_ref[0, 0, h]
        new_g = (
            whole * now_g
            - dot_tn(minus, now_g)
            + dot_tn(em_ref[0, :, h * dk : (h + 1) * dk], grad_ref[0, :, h * dv : (h + 1) * dv])
        )
        total[h] = new_g
        prod[h] = whole * now_r - dot_tn(minus, now_r)

        @pl.when(step == steps - 1)
        def _():
            pull_ref[0, h] = new_g


def backward_kernel(
    heads, dk, dv,
    q_ref, k_ref, v_ref, gb_ref, inv_ref, s_ref, p_ref, in_ref, grad_ref, g_ref, r_ref, suf_ref,
    dq_ref, dk_ref, dv_ref, dgb_ref,
):
    lane = lax.broadcasted_iota(jnp.int32, (CHUNK, CHUNK), 1)
    for h in range(heads):
        q = q_ref[0, :, h * dk : (h + 1) * dk].astype(jnp.float32)
        k = k_ref[0, :, h * dk : (h + 1) * dk].astype(jnp.float32)
        v = v_ref[0, :, h * dv : (h + 1) * dv].astype(jnp.float32)
        gate = gb_ref[0, h, :, 0:1]
        strength = gb_ref[0, h, :, 1:2]
        state = s_ref[0, 0, h].astype(jnp.float32) + dot_nn(p_ref[0, 0, h], in_ref[0, h])
        after = g_ref[0, 0, h].astype(jnp.float32) + dot_nn(r_ref[0, 0, h], suf_ref[0, h])
        inverse = inv_ref[0, 0, h]
        unused, back = jax.vjp(
            lambda *five: chunk_out(*five, inverse, state), q, k, v, gate, strength
        )
        dq, dkk, dvv, dgate, dstrength = back((grad_ref[0, :, h * dv : (h + 1) * dv], after))
        dq_ref[0, :, h * dk : (h + 1) * dk] = dq
        dk_ref[0, :, h * dk : (h + 1) * dk] = dkk
        dv_ref[0, :, h * dv : (h + 1) * dv] = dvv
        dgb_ref[0, h] = jnp.where(lane == 0, dgate, jnp.where(lane == 1, dstrength, 0.0))


def kernel_specs(heads, dk, dv, steps, reverse):
    def at(c):
        return steps - 1 - c if reverse else c

    return {
        "k": pl.BlockSpec((1, CHUNK, heads * dk), lambda s, c: (s, at(c), 0)),
        "v": pl.BlockSpec((1, CHUNK, heads * dv), lambda s, c: (s, at(c), 0)),
        "gb": pl.BlockSpec((1, heads, CHUNK, CHUNK), lambda s, c: (s, 0, at(c), 0)),
        "kk": pl.BlockSpec((1, 1, heads, dk, dk), lambda s, c: (s, at(c), 0, 0, 0)),
        "kv": pl.BlockSpec((1, 1, heads, dk, dv), lambda s, c: (s, at(c), 0, 0, 0)),
        "dkk": pl.BlockSpec((1, heads, dk, dk), lambda s, c: (s, 0, 0, 0)),
        "dkv": pl.BlockSpec((1, heads, dk, dv), lambda s, c: (s, 0, 0, 0)),
    }


def kernel_call(body, grid, ins, outs, scratch=()):
    return pl.pallas_call(
        body,
        grid=grid,
        in_specs=ins,
        out_specs=[o[0] for o in outs],
        out_shape=[jax.ShapeDtypeStruct(o[1], o[2]) for o in outs],
        scratch_shapes=list(scratch),
        compiler_params=pltpu.CompilerParams(
            dimension_semantics=("arbitrary", "arbitrary"), vmem_limit_bytes=40 * 1024 * 1024
        ),
    )


def combine_maps(earlier, later):
    return (high_dot(later[0], earlier[0]), high_dot(later[0], earlier[1]) + later[1])


def identity_maps(carry_map, carry_add):
    lane_count = carry_map.shape[0]
    key_dim = carry_map.shape[-1]
    eye_block = jnp.broadcast_to(
        jnp.eye(key_dim, dtype=jnp.float32), (lane_count, key_dim, key_dim)
    )
    return (eye_block, jnp.zeros((lane_count,) + carry_add.shape[-2:], jnp.float32))


def rows_dot(left, right):
    return lax.dot_general(
        left, right, (((0,), (0,)), ((), ())), preferred_element_type=jnp.float32
    ).astype(jnp.bfloat16)


def summed_over_rows(partial):
    return lax.psum_scatter(
        partial, ("dp", "ctx"), scatter_dimension=0, tiled=True
    ).astype(jnp.float32)


def scattered(left, right):
    return summed_over_rows(rows_dot(left, right))


def per_device(
    tokens,
    first_gain,
    query_weight,
    key_weight,
    value_weight,
    outgate_weight,
    alpha_weight,
    beta_weight,
    query_conv,
    convolved_keys,
    value_conv,
    decay_rate,
    time_bias,
    head_gain,
    out_weight,
    second_gain,
    gate_weight,
    up_weight,
    down_weight,
    cotangent,
):
    seq_count, local_len, model_width = tokens.shape
    rows = seq_count * local_len
    heads = decay_rate.shape[0]
    q_cols = query_weight.shape[1]
    k_cols = key_weight.shape[1]
    v_cols = value_weight.shape[1]
    key_dim = q_cols // heads
    val_dim = v_cols // heads
    steps = local_len // CHUNK
    lane_count = seq_count * heads

    def mixer_front(padded_in, kernel_in, alpha_in, beta_in, decay_in, bias_in):
        summed = sum(
            (
                kernel_in[tap_index] * padded_in[:, tap_index : tap_index + local_len, :]
                for tap_index in range(KCONV)
            )
        )
        active = jax.nn.silu(summed)
        def unit(first, width):
            pieces = [active[..., first + h * width : first + (h + 1) * width] for h in range(heads)]
            return jnp.concatenate(
                [p * lax.rsqrt(jnp.sum(p * p, -1, keepdims=True) + epsilon) for p in pieces], -1
            )

        unit_query = unit(0, key_dim) * key_dim ** (-0.5)
        unit_key = unit(q_cols, key_dim)
        raw_value = active[..., q_cols + k_cols :]
        log_gate = -decay_in * jax.nn.softplus(
            alpha_in.reshape(seq_count, local_len, heads) + bias_in
        )
        strength = jax.nn.sigmoid(beta_in.reshape(seq_count, local_len, heads))
        both = jnp.stack([log_gate, strength], -1)
        both = jnp.transpose(both, (0, 2, 1, 3))
        both = jnp.pad(both, ((0, 0), (0, 0), (0, 0), (0, CHUNK - 2)))
        return (unit_query, unit_key, raw_value, both)

    inputs = tokens.reshape(rows, model_width).astype(jnp.float32)
    normed1, norm1_back = jax.vjp(rms_gain, inputs, first_gain)
    normed1_b = normed1.astype(jnp.bfloat16)

    def project(weight):
        return jnp.dot(normed1_b, weight, preferred_element_type=jnp.float32)

    linear = jnp.concatenate([project(query_weight), project(key_weight), project(value_weight)], 1)
    linear = linear.astype(jnp.bfloat16).reshape(seq_count, local_len, q_cols + k_cols + v_cols)
    gate_lin = project(outgate_weight)
    alpha_lin = project(alpha_weight)
    beta_lin = project(beta_weight)
    rims = shifted(linear[:, local_len - (KCONV - 1) :, :], "ctx", 1)
    padded = jnp.concatenate([rims, linear], 1).astype(jnp.float32)
    kernel = jnp.concatenate([query_conv, convolved_keys, value_conv], 1)
    front_out, front_back = jax.vjp(
        mixer_front, padded, kernel, alpha_lin, beta_lin, decay_rate, time_bias
    )
    queries = front_out[0].astype(jnp.bfloat16)
    keys_in = front_out[1].astype(jnp.bfloat16)
    values_in = front_out[2].astype(jnp.bfloat16)
    both = front_out[3]
    grid = (seq_count, steps)
    low, full = jnp.bfloat16, jnp.float32
    k_rows, v_rows = (seq_count, local_len, q_cols), (seq_count, local_len, v_cols)
    kk = (seq_count, steps, heads, key_dim, key_dim)
    kv = (seq_count, steps, heads, key_dim, val_dim)
    dkk, dkv = (seq_count,) + kk[2:], (seq_count,) + kv[2:]
    spec = kernel_specs(heads, key_dim, val_dim, steps, False)
    carries = (
        pltpu.VMEM((heads, key_dim, val_dim), full),
        pltpu.VMEM((heads, key_dim, key_dim), full),
    )
    emitted, emitted_in, head_local, inverse, minus, states, prods, device_map, device_add = kernel_call(
        functools.partial(forward_kernel, heads, key_dim, val_dim, steps),
        grid,
        [spec["k"], spec["k"], spec["v"], spec["gb"]],
        [
            (spec["k"], k_rows, low),
            (spec["k"], k_rows, low),
            (spec["v"], v_rows, full),
            (spec["kk"], kk, low),
            (spec["kk"], kk, low),
            (spec["kv"], kv, low),
            (spec["kk"], kk, low),
            (spec["dkk"], dkk, full),
            (spec["dkv"], dkv, full),
        ],
        carries,
    )(queries, keys_in, values_in, both)
    device_map = device_map.reshape(lane_count, key_dim, key_dim)
    device_add = device_add.reshape(lane_count, key_dim, val_dim)
    prefix = entering(
        (device_map, device_add), "ctx", combine_maps, identity_maps(device_map, device_add), False
    )
    state_in = prefix[1].astype(low).reshape(dkv)
    head_out = jnp.stack(
        [
            head_local[..., h * val_dim : (h + 1) * val_dim]
            + jnp.einsum(
                "stk,skv->stv",
                emitted_in[..., h * key_dim : (h + 1) * key_dim],
                state_in[:, h],
                preferred_element_type=full,
            )
            for h in range(heads)
        ],
        2,
    )
    gate_heads = gate_lin.reshape(seq_count, local_len, heads, val_dim)
    normed_heads, gated_back = jax.vjp(gated_out, head_out, gate_heads, head_gain)
    normed_heads_b = normed_heads.reshape(rows, v_cols).astype(jnp.bfloat16)
    mixer_part = jnp.dot(normed_heads_b, out_weight, preferred_element_type=jnp.float32)
    middle = inputs + lax.psum(mixer_part.astype(jnp.bfloat16), "tensor").astype(jnp.float32)
    normed2, second_norm_backward = jax.vjp(rms_gain, middle, second_gain)
    normed2_b = normed2.astype(jnp.bfloat16)
    gate_pre = jnp.dot(normed2_b, gate_weight, preferred_element_type=jnp.float32)
    up_pre = jnp.dot(normed2_b, up_weight, preferred_element_type=jnp.float32)
    hidden_f, swiglu_back = jax.vjp(swiglu, gate_pre, up_pre)
    hidden = hidden_f.astype(jnp.bfloat16)
    ffn_part = jnp.dot(hidden, down_weight, preferred_element_type=jnp.float32)
    block_out = (
        middle + lax.psum(ffn_part.astype(jnp.bfloat16), "tensor").astype(jnp.float32)
    ).astype(jnp.bfloat16)
    grad_rows = cotangent.reshape(rows, model_width)
    hidden_grad = jnp.dot(grad_rows, down_weight.T, preferred_element_type=jnp.float32)
    gate_grad, up_grad = swiglu_back(hidden_grad)
    gate_grad_b = gate_grad.astype(jnp.bfloat16)
    up_grad_b = up_grad.astype(jnp.bfloat16)
    normed2_part = jnp.dot(gate_grad_b, gate_weight.T, preferred_element_type=jnp.float32)
    normed2_part = normed2_part + jnp.dot(
        up_grad_b, up_weight.T, preferred_element_type=jnp.float32
    )
    normed2_grad = lax.psum(normed2_part.astype(jnp.bfloat16), "tensor").astype(jnp.float32)
    middle_norm_grad, second_gain_grad = second_norm_backward(normed2_grad)
    middle_grad = grad_rows.astype(jnp.float32) + middle_norm_grad
    middle_low = middle_grad.astype(jnp.bfloat16)
    ffn_cols = gate_weight.shape[1]
    ffn_w = summed_over_rows(
        jnp.concatenate(
            [
                rows_dot(normed2_b, jnp.concatenate([gate_grad_b, up_grad_b], 1)),
                rows_dot(grad_rows, hidden),
            ],
            1,
        )
    )
    out_w = scattered(middle_low, normed_heads_b)
    heads_grad = jnp.dot(middle_low, out_weight.T, preferred_element_type=jnp.float32).reshape(
        seq_count, local_len, heads, val_dim
    )
    head_out_grad, head_gate_gradient, head_gain_grad = gated_back(heads_grad)
    out_grad = head_out_grad.reshape(v_rows)
    back_spec = kernel_specs(heads, key_dim, val_dim, steps, True)
    pulls, suffixes, local_pull = kernel_call(
        functools.partial(pull_kernel, heads, key_dim, val_dim, steps),
        grid,
        [back_spec["k"], back_spec["kk"], back_spec["gb"], back_spec["v"]],
        [
            (back_spec["kv"], kv, low),
            (back_spec["kk"], kk, low),
            (back_spec["dkv"], dkv, full),
        ],
        carries,
    )(emitted, minus, both, out_grad)
    suffix = entering(
        (flipped(device_map), local_pull.reshape(lane_count, key_dim, val_dim)),
        "ctx",
        combine_maps,
        identity_maps(device_map, device_add),
        True,
    )
    suffix_in = suffix[1].astype(low).reshape(dkv)
    query_grad, key_grad, value_grad, both_grad = kernel_call(
        functools.partial(backward_kernel, heads, key_dim, val_dim),
        grid,
        [
            spec["k"], spec["k"], spec["v"], spec["gb"], spec["kk"], spec["kv"], spec["kk"],
            spec["dkv"], spec["v"], spec["kv"], spec["kk"], spec["dkv"],
        ],
        [
            (spec["k"], k_rows, full),
            (spec["k"], k_rows, full),
            (spec["v"], v_rows, full),
            (spec["gb"], both.shape, full),
        ],
    )(
        queries, keys_in, values_in, both, inverse, states, prods,
        state_in, out_grad, pulls, suffixes, suffix_in,
    )
    padded_grad, kernel_grad, alpha_grad, beta_grad, decay_grad, bias_grad = front_back(
        (query_grad, key_grad, value_grad, both_grad)
    )
    rim_back = shifted(padded_grad[:, : KCONV - 1, :].astype(jnp.bfloat16), "ctx", -1).astype(
        jnp.float32
    )
    linear_grad = padded_grad[:, KCONV - 1 :, :] + jnp.pad(
        rim_back, ((0, 0), (local_len - (KCONV - 1), 0), (0, 0))
    )
    linear_grad_b = linear_grad.reshape(rows, q_cols + k_cols + v_cols).astype(jnp.bfloat16)
    query_lin_grad = linear_grad_b[:, :q_cols]
    key_lin_grad = linear_grad_b[:, q_cols : q_cols + k_cols]
    value_lin_grad = linear_grad_b[:, q_cols + k_cols :]
    gate_lin_grad = head_gate_gradient.reshape(rows, v_cols).astype(jnp.bfloat16)
    alpha_lin_grad = alpha_grad.astype(jnp.bfloat16)
    beta_lin_grad = beta_grad.astype(jnp.bfloat16)
    paired = (
        (query_weight, query_lin_grad),
        (key_weight, key_lin_grad),
        (value_weight, value_lin_grad),
        (outgate_weight, gate_lin_grad),
        (alpha_weight, alpha_lin_grad),
        (beta_weight, beta_lin_grad),
    )
    normed1_part = sum(
        (jnp.dot(grad_b, weight.T, preferred_element_type=jnp.float32) for weight, grad_b in paired)
    )
    late_cols = jnp.concatenate([linear_grad_b, alpha_lin_grad, beta_lin_grad], 1)
    late_w = scattered(normed1_b, late_cols)
    gate_w = scattered(normed1_b, gate_lin_grad)
    normed1_grad = lax.psum(normed1_part.astype(jnp.bfloat16), "tensor").astype(jnp.float32)
    inputs_norm_grad, first_gain_grad = norm1_back(normed1_grad)
    tokens_grad = (middle_grad + inputs_norm_grad).astype(jnp.bfloat16)
    v_end = q_cols + k_cols + v_cols
    weight_grads = (
        late_w[:, :q_cols],
        late_w[:, q_cols : q_cols + k_cols],
        late_w[:, q_cols + k_cols : v_end],
        gate_w,
        late_w[:, v_end : v_end + heads],
        late_w[:, v_end + heads :],
        out_w.T,
        ffn_w[:, :ffn_cols],
        ffn_w[:, ffn_cols : 2 * ffn_cols],
        ffn_w[:, 2 * ffn_cols :].T,
    )
    index = lax.axis_index("tensor")
    first_own = jnp.where(index == 0, 1.0, 0.0)
    gains = lax.psum(
        jnp.concatenate([first_own * first_gain_grad, first_own * second_gain_grad, head_gain_grad]),
        ("dp", "ctx", "tensor"),
    )
    smalls = lax.psum(
        jnp.concatenate([kernel_grad.reshape(-1), decay_grad, bias_grad]), ("dp", "ctx")
    )
    taps = kernel_grad.size
    small_sums = (
        gains[:model_width],
        gains[model_width : 2 * model_width],
        gains[2 * model_width :],
        smalls[:taps].reshape(kernel_grad.shape),
        smalls[taps : taps + heads],
        smalls[taps + heads :],
    )
    kernel_sum = small_sums[3]
    return (
        block_out.reshape(seq_count, local_len, model_width),
        tokens_grad.reshape(seq_count, local_len, model_width),
        small_sums[0],
        weight_grads[0],
        weight_grads[1],
        weight_grads[2],
        weight_grads[3],
        weight_grads[4],
        weight_grads[5],
        kernel_sum[:, :q_cols],
        kernel_sum[:, q_cols : q_cols + k_cols],
        kernel_sum[:, q_cols + k_cols :],
        small_sums[4],
        small_sums[5],
        small_sums[2],
        weight_grads[6],
        small_sums[1],
        weight_grads[7],
        weight_grads[8],
        weight_grads[9],
    )


def solution(mesh):
    placed = (
        P("dp", "ctx", None),
        P(),
        P(None, "tensor"),
        P(None, "tensor"),
        P(None, "tensor"),
        P(None, "tensor"),
        P(None, "tensor"),
        P(None, "tensor"),
        P(None, "tensor"),
        P(None, "tensor"),
        P(None, "tensor"),
        P("tensor"),
        P("tensor"),
        P(),
        P("tensor", None),
        P(),
        P(None, "tensor"),
        P(None, "tensor"),
        P("tensor", None),
        P("dp", "ctx", None),
    )
    return jax.shard_map(
        per_device,
        mesh=mesh,
        in_specs=placed,
        out_specs=(
            P("dp", "ctx", None),
            P("dp", "ctx", None),
            P(),
            P(("dp", "ctx"), "tensor"),
            P(("dp", "ctx"), "tensor"),
            P(("dp", "ctx"), "tensor"),
            P(("dp", "ctx"), "tensor"),
            P(("dp", "ctx"), "tensor"),
            P(("dp", "ctx"), "tensor"),
            P(None, "tensor"),
            P(None, "tensor"),
            P(None, "tensor"),
            P("tensor"),
            P("tensor"),
            P(),
            P("tensor", ("dp", "ctx")),
            P(),
            P(("dp", "ctx"), "tensor"),
            P(("dp", "ctx"), "tensor"),
            P("tensor", ("dp", "ctx")),
        ),
        check_vma=False,
    )
```

```python
import functools

import jax
import jax.numpy as jnp
from jax import lax
from jax.experimental import pallas as pl
from jax.experimental.pallas import tpu as pltpu
from jax.sharding import PartitionSpec as P

KCONV = 4
CHUNK = 128


epsilon = 1e-06
maximal_precision = lax.Precision.HIGHEST


def shifted(value, axis, by):
    devices = lax.axis_size(axis)
    pairs = [(i, i + by) for i in range(devices) if 0 <= i + by < devices]
    return lax.ppermute(value, axis, pairs)


def entering(carry_map, carry_add, axis, reverse):
    devices = lax.axis_size(axis)
    sign = -1 if reverse else 1
    map_low, add_low = carry_map.astype(jnp.bfloat16), carry_add.astype(jnp.bfloat16)
    state = None
    for away in range(devices - 1, 0, -1):
        added = shifted(add_low, axis, sign * away).astype(jnp.float32)
        if state is None:
            state = added
        else:
            state = high_dot(shifted(map_low, axis, sign * away).astype(jnp.float32), state) + added
    return jnp.zeros_like(carry_add) if state is None else state


def high_dot(left, right):
    return jnp.matmul(left, right, precision=maximal_precision)


def flipped(matrix):
    return jnp.swapaxes(matrix, -1, -2)


def span_first(array_in):
    return jnp.moveaxis(array_in, 1, 0)


def rms_gain(rows_in, gain_in):
    return rows_in * lax.rsqrt(jnp.mean(rows_in * rows_in, -1, keepdims=True) + epsilon) * gain_in


def gated_out(head_vals, gate_vals, gain_in):
    return rms_gain(head_vals, gain_in) * jax.nn.silu(gate_vals)


def swiglu(gate_in, up_in):
    return jax.nn.silu(gate_in) * up_in


def dims_dot(left, right, left_dim, right_dim):
    return lax.dot_general(
        left.astype(jnp.bfloat16),
        right.astype(jnp.bfloat16),
        (((left_dim,), (right_dim,)), ((), ())),
        preferred_element_type=jnp.float32,
    )


@jax.custom_vjp
def dot_nn(left, right):
    return dims_dot(left, right, 1, 0)


@jax.custom_vjp
def dot_nt(left, right):
    return dims_dot(left, right, 1, 1)


@jax.custom_vjp
def dot_tn(left, right):
    return dims_dot(left, right, 0, 0)


dot_nn.defvjp(
    lambda l, r: (dims_dot(l, r, 1, 0), (l, r)),
    lambda k, g: (dims_dot(g, k[1], 1, 1), dims_dot(k[0], g, 0, 0)),
)
dot_nt.defvjp(
    lambda l, r: (dims_dot(l, r, 1, 1), (l, r)),
    lambda k, g: (dims_dot(g, k[1], 1, 0), dims_dot(g, k[0], 0, 0)),
)
dot_tn.defvjp(
    lambda l, r: (dims_dot(l, r, 0, 0), (l, r)),
    lambda k, g: (dims_dot(k[1], g, 1, 1), dims_dot(k[0], g, 1, 0)),
)


@jax.custom_vjp
def solve_with(lower, inverse, right):
    return dims_dot(inverse, right, 1, 0)


def solve_fwd(lower, inverse, right):
    found = dims_dot(inverse, right, 1, 0)
    return found, (inverse, found)


def solve_bwd(kept, grad):
    inverse, found = kept
    right_grad = dims_dot(inverse, grad, 0, 0)
    return -dims_dot(right_grad, found, 1, 1), jnp.zeros_like(inverse), right_grad


solve_with.defvjp(solve_fwd, solve_bwd)


def two_parts(value):
    high = value.astype(jnp.bfloat16)
    return high, (value - high.astype(jnp.float32)).astype(jnp.bfloat16)


def grid_indices():
    shape = (CHUNK, CHUNK)
    return lax.broadcasted_iota(jnp.int32, shape, 0), lax.broadcasted_iota(jnp.int32, shape, 1)


def triangle(flip):
    row, col = grid_indices()
    keep = row <= col if flip else row >= col
    return jnp.where(keep, 1.0, 0.0).astype(jnp.bfloat16)


def tri_dot(value, flip):
    tri = triangle(flip)
    high, rest = two_parts(value)
    return dims_dot(tri, high, 1, 0) + dims_dot(tri, rest, 1, 0)


@jax.custom_vjp
def running(value):
    return tri_dot(value, False)


running.defvjp(lambda v: (tri_dot(v, False), None), lambda k, g: (tri_dot(g, True),))


def dot_three(left, right):
    left_high, left_rest = two_parts(left)
    right_high, right_rest = two_parts(right)
    return (
        dims_dot(left_high, right_high, 1, 0)
        + dims_dot(left_high, right_rest, 1, 0)
        + dims_dot(left_rest, right_high, 1, 0)
    )


def unit_inverse(lowers):
    row, col = grid_indices()
    eye = jnp.where(row == col, 1.0, 0.0)
    found = None
    size = 1
    while size < CHUNK:
        pair = (
            (row // (2 * size) == col // (2 * size))
            & (row % (2 * size) >= size)
            & (col % (2 * size) < size)
        )
        corners = [jnp.where(pair, lower, 0.0) for lower in lowers]
        if found is None:
            found = [eye - corner for corner in corners]
        else:
            inner = [dot_three(x, c) for x, c in zip(found, corners)]
            found = [x - dot_three(i, x) for x, i in zip(found, inner)]
        size *= 2
    return found


def decay_parts(gate):
    row, col = grid_indices()
    total = running(gate * jnp.ones((CHUNK, CHUNK), jnp.float32))
    causal = row >= col
    ratio = total - total.T
    decays = jnp.where(causal, jnp.exp(jnp.where(causal, ratio, 0.0)), 0.0)
    last = jnp.sum(jnp.where(row == CHUNK - 1, total, 0.0), 0, keepdims=True)
    tails = jnp.exp(last - total)
    whole = jnp.exp(jnp.sum(gate, 0, keepdims=True))
    return decays, jnp.exp(total), tails, whole


def lower_of(decays, keys, strength):
    row, col = grid_indices()
    return jnp.where(row > col, decays * dot_nt(keys, keys), 0.0) * strength


def chunk_out(queries, keys, values, gate, strength, inverse, state):
    decays, gammas, tails, whole = decay_parts(gate)
    lower = lower_of(decays, keys, strength)
    right = strength * (values - dot_nn(gammas * keys, state))
    fresh = solve_with(lower, inverse, right)
    out = dot_nn(gammas * queries, state) + dot_nn(decays * dot_nt(queries, keys), fresh)
    return out, whole * state + dot_tn(tails * keys, fresh)


def forward_kernel(
    heads, dk, dv, steps,
    q_ref, k_ref, v_ref, gb_ref,
    em_ref, ep_ref, out_ref, inv_ref, mt_ref, s_ref, p_ref, dmap_ref, dadd_ref,
    state, prod,
):
    step = pl.program_id(1)

    @pl.when(step == 0)
    def _():
        row, col = grid_indices()
        state[...] = jnp.zeros_like(state)
        for h in range(heads):
            prod[h] = jnp.where(row == col, 1.0, 0.0)

    parts, lowers = [], []
    for h in range(heads):
        q = q_ref[0, :, h * dk : (h + 1) * dk].astype(jnp.float32)
        k = k_ref[0, :, h * dk : (h + 1) * dk].astype(jnp.float32)
        v = v_ref[0, :, h * dv : (h + 1) * dv].astype(jnp.float32)
        gate = gb_ref[0, :, h : h + 1]
        strength = gb_ref[0, :, heads + h : heads + h + 1]
        decays, gammas, tails, whole = decay_parts(gate)
        lowers.append(lower_of(decays, k, strength))
        parts.append((q, k, v, strength, decays, gammas, tails, whole))
    inverses = unit_inverse(lowers)
    for h in range(heads):
        q, k, v, strength, decays, gammas, tails, whole = parts[h]
        inverse = inverses[h].astype(jnp.bfloat16)
        key_solve = dot_nn(inverse, strength * gammas * k)
        value_solve = dot_nn(inverse, strength * v)
        mixing = decays * dot_nt(q, k)
        emitted = (gammas * q - dot_nn(mixing, key_solve)).astype(jnp.bfloat16)
        tail_keys = tails * k
        minus = dot_tn(tail_keys, key_solve).astype(jnp.bfloat16)
        now_s, now_p = state[h], prod[h]
        inv_ref[0, 0, h] = inverse
        mt_ref[0, 0, h] = minus
        s_ref[0, 0, h] = now_s.astype(jnp.bfloat16)
        p_ref[0, 0, h] = now_p.astype(jnp.bfloat16)
        em_ref[0, :, h * dk : (h + 1) * dk] = emitted
        ep_ref[0, :, h * dk : (h + 1) * dk] = dot_nn(emitted, now_p).astype(jnp.bfloat16)
        out_ref[0, :, h * dv : (h + 1) * dv] = dot_nn(mixing, value_solve) + dot_nn(emitted, now_s)
        new_s = whole * now_s - dot_nn(minus, now_s) + dot_tn(tail_keys, value_solve)
        new_p = whole * now_p - dot_nn(minus, now_p)
        state[h] = new_s
        prod[h] = new_p

        @pl.when(step == steps - 1)
        def _():
            dmap_ref[0, h] = new_p
            dadd_ref[0, h] = new_s


def pull_kernel(
    heads, dk, dv, steps,
    em_ref, mt_ref, gb_ref, grad_ref,
    g_ref, r_ref, pull_ref,
    total, prod,
):
    step = pl.program_id(1)

    @pl.when(step == 0)
    def _():
        row, col = grid_indices()
        total[...] = jnp.zeros_like(total)
        for h in range(heads):
            prod[h] = jnp.where(row == col, 1.0, 0.0)

    for h in range(heads):
        whole = jnp.exp(jnp.sum(gb_ref[0, :, h : h + 1], 0, keepdims=True))
        now_g, now_r = total[h], prod[h]
        g_ref[0, 0, h] = now_g.astype(jnp.bfloat16)
        r_ref[0, 0, h] = now_r.astype(jnp.bfloat16)
        minus = mt_ref[0, 0, h]
        new_g = (
            whole * now_g
            - dot_tn(minus, now_g)
            + dot_tn(em_ref[0, :, h * dk : (h + 1) * dk], grad_ref[0, :, h * dv : (h + 1) * dv])
        )
        total[h] = new_g
        prod[h] = whole * now_r - dot_tn(minus, now_r)

        @pl.when(step == steps - 1)
        def _():
            pull_ref[0, h] = new_g


def backward_kernel(
    heads, dk, dv,
    q_ref, k_ref, v_ref, gb_ref, inv_ref, s_ref, p_ref, in_ref, grad_ref, g_ref, r_ref, suf_ref,
    dq_ref, dk_ref, dv_ref, dgb_ref,
):
    lane = lax.broadcasted_iota(jnp.int32, (CHUNK, CHUNK), 1)
    packed = jnp.zeros((CHUNK, CHUNK), jnp.float32)
    for h in range(heads):
        q = q_ref[0, :, h * dk : (h + 1) * dk].astype(jnp.float32)
        k = k_ref[0, :, h * dk : (h + 1) * dk].astype(jnp.float32)
        v = v_ref[0, :, h * dv : (h + 1) * dv].astype(jnp.float32)
        gate = gb_ref[0, :, h : h + 1]
        strength = gb_ref[0, :, heads + h : heads + h + 1]
        state = s_ref[0, 0, h].astype(jnp.float32) + dot_nn(p_ref[0, 0, h], in_ref[0, h])
        after = g_ref[0, 0, h].astype(jnp.float32) + dot_nn(r_ref[0, 0, h], suf_ref[0, h])
        inverse = inv_ref[0, 0, h]
        unused, back = jax.vjp(
            lambda *five: chunk_out(*five, inverse, state), q, k, v, gate, strength
        )
        dq, dkk, dvv, dgate, dstrength = back((grad_ref[0, :, h * dv : (h + 1) * dv], after))
        dq_ref[0, :, h * dk : (h + 1) * dk] = dq
        dk_ref[0, :, h * dk : (h + 1) * dk] = dkk
        dv_ref[0, :, h * dv : (h + 1) * dv] = dvv
        packed = jnp.where(lane == h, dgate, jnp.where(lane == heads + h, dstrength, packed))
    dgb_ref[0] = packed


def kernel_specs(heads, dk, dv, steps, reverse):
    def at(c):
        return steps - 1 - c if reverse else c

    return {
        "k": pl.BlockSpec((1, CHUNK, heads * dk), lambda s, c: (s, at(c), 0)),
        "v": pl.BlockSpec((1, CHUNK, heads * dv), lambda s, c: (s, at(c), 0)),
        "gb": pl.BlockSpec((1, CHUNK, CHUNK), lambda s, c: (s, at(c), 0)),
        "kk": pl.BlockSpec((1, 1, heads, dk, dk), lambda s, c: (s, at(c), 0, 0, 0)),
        "kv": pl.BlockSpec((1, 1, heads, dk, dv), lambda s, c: (s, at(c), 0, 0, 0)),
        "dkk": pl.BlockSpec((1, heads, dk, dk), lambda s, c: (s, 0, 0, 0)),
        "dkv": pl.BlockSpec((1, heads, dk, dv), lambda s, c: (s, 0, 0, 0)),
    }


def kernel_call(body, grid, ins, outs, scratch=()):
    return pl.pallas_call(
        body,
        grid=grid,
        in_specs=ins,
        out_specs=[o[0] for o in outs],
        out_shape=[jax.ShapeDtypeStruct(o[1], o[2]) for o in outs],
        scratch_shapes=list(scratch),
        compiler_params=pltpu.CompilerParams(
            dimension_semantics=("arbitrary", "arbitrary"), vmem_limit_bytes=40 * 1024 * 1024
        ),
    )


def rows_dot(left, right):
    return lax.dot_general(
        left, right, (((0,), (0,)), ((), ())), preferred_element_type=jnp.float32
    ).astype(jnp.bfloat16)


def summed_over_rows(partial):
    return lax.psum_scatter(
        partial, ("dp", "ctx"), scatter_dimension=0, tiled=True
    ).astype(jnp.float32)


def scattered(left, right):
    return summed_over_rows(rows_dot(left, right))


def per_device(
    tokens,
    first_gain,
    query_weight,
    key_weight,
    value_weight,
    outgate_weight,
    alpha_weight,
    beta_weight,
    query_conv,
    convolved_keys,
    value_conv,
    decay_rate,
    time_bias,
    head_gain,
    out_weight,
    second_gain,
    gate_weight,
    up_weight,
    down_weight,
    cotangent,
):
    seq_count, local_len, model_width = tokens.shape
    rows = seq_count * local_len
    heads = decay_rate.shape[0]
    q_cols = query_weight.shape[1]
    k_cols = key_weight.shape[1]
    v_cols = value_weight.shape[1]
    key_dim = q_cols // heads
    val_dim = v_cols // heads
    steps = local_len // CHUNK
    lane_count = seq_count * heads

    def mixer_front(padded_in, kernel_in, alpha_in, beta_in, decay_in, bias_in):
        summed = sum(
            (
                kernel_in[tap_index] * padded_in[:, tap_index : tap_index + local_len, :]
                for tap_index in range(KCONV)
            )
        )
        active = jax.nn.silu(summed)
        def unit(first, width):
            pieces = [active[..., first + h * width : first + (h + 1) * width] for h in range(heads)]
            return jnp.concatenate(
                [p * lax.rsqrt(jnp.sum(p * p, -1, keepdims=True) + epsilon) for p in pieces], -1
            )

        unit_query = unit(0, key_dim) * key_dim ** (-0.5)
        unit_key = unit(q_cols, key_dim)
        raw_value = active[..., q_cols + k_cols :]
        log_gate = -decay_in * jax.nn.softplus(
            alpha_in.reshape(seq_count, local_len, heads) + bias_in
        )
        strength = jax.nn.sigmoid(beta_in.reshape(seq_count, local_len, heads))
        both = jnp.concatenate([log_gate, strength], -1)
        both = jnp.pad(both, ((0, 0), (0, 0), (0, CHUNK - 2 * heads)))
        return (unit_query, unit_key, raw_value, both)

    inputs = tokens.reshape(rows, model_width).astype(jnp.float32)
    normed1, norm1_back = jax.vjp(rms_gain, inputs, first_gain)
    normed1_b = normed1.astype(jnp.bfloat16)

    def project(weight):
        return jnp.dot(normed1_b, weight, preferred_element_type=jnp.float32)

    linear = jnp.concatenate([project(query_weight), project(key_weight), project(value_weight)], 1)
    linear = linear.astype(jnp.bfloat16).reshape(seq_count, local_len, q_cols + k_cols + v_cols)
    gate_lin = project(outgate_weight)
    alpha_lin = project(alpha_weight)
    beta_lin = project(beta_weight)
    rims = shifted(linear[:, local_len - (KCONV - 1) :, :], "ctx", 1)
    padded = jnp.concatenate([rims, linear], 1).astype(jnp.float32)
    kernel = jnp.concatenate([query_conv, convolved_keys, value_conv], 1)
    front_out, front_back = jax.vjp(
        mixer_front, padded, kernel, alpha_lin, beta_lin, decay_rate, time_bias
    )
    queries = front_out[0].astype(jnp.bfloat16)
    keys_in = front_out[1].astype(jnp.bfloat16)
    values_in = front_out[2].astype(jnp.bfloat16)
    both = front_out[3]
    grid = (seq_count, steps)
    low, full = jnp.bfloat16, jnp.float32
    k_rows, v_rows = (seq_count, local_len, q_cols), (seq_count, local_len, v_cols)
    kk = (seq_count, steps, heads, key_dim, key_dim)
    kv = (seq_count, steps, heads, key_dim, val_dim)
    dkk, dkv = (seq_count,) + kk[2:], (seq_count,) + kv[2:]
    spec = kernel_specs(heads, key_dim, val_dim, steps, False)
    carries = (
        pltpu.VMEM((heads, key_dim, val_dim), full),
        pltpu.VMEM((heads, key_dim, key_dim), full),
    )
    emitted, emitted_in, head_local, inverse, minus, states, prods, device_map, device_add = kernel_call(
        functools.partial(forward_kernel, heads, key_dim, val_dim, steps),
        grid,
        [spec["k"], spec["k"], spec["v"], spec["gb"]],
        [
            (spec["k"], k_rows, low),
            (spec["k"], k_rows, low),
            (spec["v"], v_rows, full),
            (spec["kk"], kk, low),
            (spec["kk"], kk, low),
            (spec["kv"], kv, low),
            (spec["kk"], kk, low),
            (spec["dkk"], dkk, full),
            (spec["dkv"], dkv, full),
        ],
        carries,
    )(queries, keys_in, values_in, both)
    device_map = device_map.reshape(lane_count, key_dim, key_dim)
    device_add = device_add.reshape(lane_count, key_dim, val_dim)
    prefix = entering(device_map, device_add, "ctx", False)
    state_in = prefix.astype(low).reshape(dkv)
    head_out = jnp.stack(
        [
            head_local[..., h * val_dim : (h + 1) * val_dim]
            + jnp.einsum(
                "stk,skv->stv",
                emitted_in[..., h * key_dim : (h + 1) * key_dim],
                state_in[:, h],
                preferred_element_type=full,
            )
            for h in range(heads)
        ],
        2,
    )
    gate_heads = gate_lin.reshape(seq_count, local_len, heads, val_dim)
    normed_heads, gated_back = jax.vjp(gated_out, head_out, gate_heads, head_gain)
    normed_heads_b = normed_heads.reshape(rows, v_cols).astype(jnp.bfloat16)
    mixer_part = jnp.dot(normed_heads_b, out_weight, preferred_element_type=jnp.float32)
    middle = inputs + lax.psum(mixer_part.astype(jnp.bfloat16), "tensor").astype(jnp.float32)
    normed2, second_norm_backward = jax.vjp(rms_gain, middle, second_gain)
    normed2_b = normed2.astype(jnp.bfloat16)
    gate_pre = jnp.dot(normed2_b, gate_weight, preferred_element_type=jnp.float32)
    up_pre = jnp.dot(normed2_b, up_weight, preferred_element_type=jnp.float32)
    hidden_f, swiglu_back = jax.vjp(swiglu, gate_pre, up_pre)
    hidden = hidden_f.astype(jnp.bfloat16)
    ffn_part = jnp.dot(hidden, down_weight, preferred_element_type=jnp.float32)
    grad_rows = cotangent.reshape(rows, model_width)
    hidden_grad = jnp.dot(grad_rows, down_weight.T, preferred_element_type=jnp.float32)
    gate_grad, up_grad = swiglu_back(hidden_grad)
    gate_grad_b = gate_grad.astype(jnp.bfloat16)
    up_grad_b = up_grad.astype(jnp.bfloat16)
    normed2_part = jnp.dot(gate_grad_b, gate_weight.T, preferred_element_type=jnp.float32)
    normed2_part = normed2_part + jnp.dot(
        up_grad_b, up_weight.T, preferred_element_type=jnp.float32
    )
    normed2_grad = lax.psum(normed2_part.astype(jnp.bfloat16), "tensor").astype(jnp.float32)
    middle_norm_grad, second_gain_grad = second_norm_backward(normed2_grad)
    middle_grad = grad_rows.astype(jnp.float32) + middle_norm_grad
    middle_low = middle_grad.astype(jnp.bfloat16)
    ffn_cols = gate_weight.shape[1]
    ffn_rows = jnp.concatenate(
        [
            rows_dot(normed2_b, jnp.concatenate([gate_grad_b, up_grad_b], 1)),
            rows_dot(grad_rows, hidden),
        ],
        1,
    )
    ffn_rows, ffn_low, middle_low = lax.optimization_barrier(
        (ffn_rows, ffn_part.astype(jnp.bfloat16), middle_low)
    )
    ffn_sum = lax.psum(ffn_low, "tensor")
    ffn_w = summed_over_rows(ffn_rows)
    out_w = scattered(middle_low, normed_heads_b)
    heads_grad = jnp.dot(middle_low, out_weight.T, preferred_element_type=jnp.float32).reshape(
        seq_count, local_len, heads, val_dim
    )
    head_out_grad, head_gate_gradient, head_gain_grad = gated_back(heads_grad)
    out_grad = head_out_grad.reshape(v_rows)
    gate_lin_grad = head_gate_gradient.reshape(rows, v_cols).astype(jnp.bfloat16)
    gate_w = scattered(normed1_b, gate_lin_grad)
    back_spec = kernel_specs(heads, key_dim, val_dim, steps, True)
    pulls, suffixes, local_pull = kernel_call(
        functools.partial(pull_kernel, heads, key_dim, val_dim, steps),
        grid,
        [back_spec["k"], back_spec["kk"], back_spec["gb"], back_spec["v"]],
        [
            (back_spec["kv"], kv, low),
            (back_spec["kk"], kk, low),
            (back_spec["dkv"], dkv, full),
        ],
        carries,
    )(emitted, minus, both, out_grad)
    suffix = entering(
        flipped(device_map), local_pull.reshape(lane_count, key_dim, val_dim), "ctx", True
    )
    suffix_in = suffix.astype(low).reshape(dkv)
    query_grad, key_grad, value_grad, both_grad = kernel_call(
        functools.partial(backward_kernel, heads, key_dim, val_dim),
        grid,
        [
            spec["k"], spec["k"], spec["v"], spec["gb"], spec["kk"], spec["kv"], spec["kk"],
            spec["dkv"], spec["v"], spec["kv"], spec["kk"], spec["dkv"],
        ],
        [
            (spec["k"], k_rows, full),
            (spec["k"], k_rows, full),
            (spec["v"], v_rows, full),
            (spec["gb"], both.shape, full),
        ],
    )(
        queries, keys_in, values_in, both, inverse, states, prods,
        state_in, out_grad, pulls, suffixes, suffix_in,
    )
    query_grad, key_grad, value_grad, both_grad, ffn_w = lax.optimization_barrier(
        (query_grad, key_grad, value_grad, both_grad, ffn_w)
    )
    padded_grad, kernel_grad, alpha_grad, beta_grad, decay_grad, bias_grad = front_back(
        (query_grad, key_grad, value_grad, both_grad)
    )
    rim_back = shifted(padded_grad[:, : KCONV - 1, :].astype(jnp.bfloat16), "ctx", -1).astype(
        jnp.float32
    )
    linear_grad = padded_grad[:, KCONV - 1 :, :] + jnp.pad(
        rim_back, ((0, 0), (local_len - (KCONV - 1), 0), (0, 0))
    )
    linear_grad_b = linear_grad.reshape(rows, q_cols + k_cols + v_cols).astype(jnp.bfloat16)
    query_lin_grad = linear_grad_b[:, :q_cols]
    key_lin_grad = linear_grad_b[:, q_cols : q_cols + k_cols]
    value_lin_grad = linear_grad_b[:, q_cols + k_cols :]
    alpha_lin_grad = alpha_grad.astype(jnp.bfloat16)
    beta_lin_grad = beta_grad.astype(jnp.bfloat16)
    paired = (
        (query_weight, query_lin_grad),
        (key_weight, key_lin_grad),
        (value_weight, value_lin_grad),
        (outgate_weight, gate_lin_grad),
        (alpha_weight, alpha_lin_grad),
        (beta_weight, beta_lin_grad),
    )
    normed1_part = sum(
        (jnp.dot(grad_b, weight.T, preferred_element_type=jnp.float32) for weight, grad_b in paired)
    )
    late_cols = jnp.concatenate([linear_grad_b, alpha_lin_grad, beta_lin_grad], 1)
    late_w = scattered(normed1_b, late_cols)
    normed1_low, ffn_sum, out_w, gate_w = lax.optimization_barrier(
        (normed1_part.astype(jnp.bfloat16), ffn_sum, out_w, gate_w)
    )
    block_out = (middle + ffn_sum.astype(jnp.float32)).astype(jnp.bfloat16)
    normed1_grad = lax.psum(normed1_low, "tensor").astype(jnp.float32)
    inputs_norm_grad, first_gain_grad = norm1_back(normed1_grad)
    tokens_grad = (middle_grad + inputs_norm_grad).astype(jnp.bfloat16)
    v_end = q_cols + k_cols + v_cols
    weight_grads = (
        late_w[:, :q_cols],
        late_w[:, q_cols : q_cols + k_cols],
        late_w[:, q_cols + k_cols : v_end],
        gate_w,
        late_w[:, v_end : v_end + heads],
        late_w[:, v_end + heads :],
        out_w.T,
        ffn_w[:, :ffn_cols],
        ffn_w[:, ffn_cols : 2 * ffn_cols],
        ffn_w[:, 2 * ffn_cols :].T,
    )
    index = lax.axis_index("tensor")
    first_own = jnp.where(index == 0, 1.0, 0.0)
    gains = jnp.sum(
        lax.all_gather(
            jnp.concatenate(
                [first_own * first_gain_grad, first_own * second_gain_grad, head_gain_grad]
            ),
            ("dp", "ctx", "tensor"),
        ),
        0,
    )
    own = jnp.concatenate([kernel_grad.reshape(-1), decay_grad, bias_grad])
    own = jnp.pad(own, (0, -own.size % 1024))
    smalls = jnp.sum(lax.all_gather(own, ("dp", "ctx")), 0)
    taps = kernel_grad.size
    small_sums = (
        gains[:model_width],
        gains[model_width : 2 * model_width],
        gains[2 * model_width :],
        smalls[:taps].reshape(kernel_grad.shape),
        smalls[taps : taps + heads],
        smalls[taps + heads : taps + 2 * heads],
    )
    kernel_sum = small_sums[3]
    return (
        block_out.reshape(seq_count, local_len, model_width),
        tokens_grad.reshape(seq_count, local_len, model_width),
        small_sums[0],
        weight_grads[0],
        weight_grads[1],
        weight_grads[2],
        weight_grads[3],
        weight_grads[4],
        weight_grads[5],
        kernel_sum[:, :q_cols],
        kernel_sum[:, q_cols : q_cols + k_cols],
        kernel_sum[:, q_cols + k_cols :],
        small_sums[4],
        small_sums[5],
        small_sums[2],
        weight_grads[6],
        small_sums[1],
        weight_grads[7],
        weight_grads[8],
        weight_grads[9],
    )


def solution(mesh):
    placed = (
        P("dp", "ctx", None),
        P(),
        P(None, "tensor"),
        P(None, "tensor"),
        P(None, "tensor"),
        P(None, "tensor"),
        P(None, "tensor"),
        P(None, "tensor"),
        P(None, "tensor"),
        P(None, "tensor"),
        P(None, "tensor"),
        P("tensor"),
        P("tensor"),
        P(),
        P("tensor", None),
        P(),
        P(None, "tensor"),
        P(None, "tensor"),
        P("tensor", None),
        P("dp", "ctx", None),
    )
    return jax.shard_map(
        per_device,
        mesh=mesh,
        in_specs=placed,
        out_specs=(
            P("dp", "ctx", None),
            P("dp", "ctx", None),
            P(),
            P(("dp", "ctx"), "tensor"),
            P(("dp", "ctx"), "tensor"),
            P(("dp", "ctx"), "tensor"),
            P(("dp", "ctx"), "tensor"),
            P(("dp", "ctx"), "tensor"),
            P(("dp", "ctx"), "tensor"),
            P(None, "tensor"),
            P(None, "tensor"),
            P(None, "tensor"),
            P("tensor"),
            P("tensor"),
            P(),
            P("tensor", ("dp", "ctx")),
            P(),
            P(("dp", "ctx"), "tensor"),
            P(("dp", "ctx"), "tensor"),
            P("tensor", ("dp", "ctx")),
        ),
        check_vma=False,
    )
```
